32 devices in a mesh: rep: 4 (over z), tp: 8 (over y, x, core).
Axes of the slice: x: 2, y: 2, z: 4, core: 2. Of those that a mesh axis runs over, the one named last changes fastest.
Arguments:
- tokens: bfloat16 [2048, 8192], P('rep', 'tp'), may hold values from -17 to 17
- query_weight: bfloat16 [8192, 8192], P(('rep', 'tp')), may hold values from -0.0625 to 0.0625
- output_weight: bfloat16 [8192, 8192], P(('rep', 'tp')), may hold values from -0.0625 to 0.0625
- keyval_slot: bfloat16 [4, 8, 8192, 256], P('rep', 'tp'), may hold values from -0.0625 to 0.0625
- holder: int32 [8], replicated, may hold values from 0 to 3, as said below
Outputs:
- query_local: bfloat16 [8192, 8192], P(None, 'tp')
- output_local: bfloat16 [8192, 8192], P(None, 'tp')
- keyval_local: bfloat16 [8, 8192, 256], P('tp')
- attended: bfloat16 [2048, 8192], P(('rep', 'tp'))
The draws below stay inside these ranges and needn't reach their ends.
Inputs may be any that keep to these rules, and one draw needn't show every extreme that they name: Key-value head h is held at replica holder[h] // 1 and tensor rank 1 * h + holder[h] % 1.
All inputs are finite; a program needn't handle non-finite values.
Results may differ from the reference program's by a relative error of at most 0.019.
The reference program's roundings to bfloat16 on the way count: a program that leaves them out, or rounds other values in their place, can miss the bound.
Values may be sent and summed in bfloat16 or wider, within the bound.
A program may use at most 192 MiB of HBM per device.

```python
import math
import jax
import jax.numpy as jnp
from jax import lax

D = 8192
HD = 128
HQW = 64
KVH = 8
TOK = 512
COLS = 8192
N_REP = 4
N_TP = 8


def draw_tokens(key, part):
    first = jax.random.fold_in(key, 0)
    rows_all = N_REP * TOK
    base = jax.random.normal(first, (rows_all, D), jnp.float32)
    return jnp.clip(base, -6.0, 6.0).astype(jnp.bfloat16)


def draw_holder(key, part):
    top_value = N_REP * (N_TP // KVH)
    first, second = jax.random.split(key)
    picks = jax.random.randint(first, (KVH,), 0, top_value)
    order = jax.random.permutation(second, KVH)
    picks = picks.at[order[0]].set(top_value - 1)
    picks = picks.at[order[1]].set(0)
    return picks.astype(jnp.int32)


def block_scale(key, shape, cuts, smallest, high):
    gain, own = 1.0, jax.random.fold_in(key, 6)
    for position, blocks in cuts:
        heights = jnp.exp(jax.random.uniform(jax.random.fold_in(own, position), (blocks,), jnp.float32, smallest / len(cuts), high / len(cuts)))
        gain = gain * jnp.repeat(heights, shape[position] // blocks).reshape([-1 if axis == position else 1 for axis in range(len(shape))])
    return gain


def bell_draw(own_key, extent, deviation, reach, cuts=(), held_as=jnp.bfloat16):
    drawn = jax.random.normal(own_key, extent, jnp.float32) * deviation
    if len(cuts) > 0:
        drawn = block_scale(own_key, extent, cuts, -0.22, 0.18) * drawn
    return jnp.clip(drawn, min=-reach, max=reach).astype(held_as)


def setup_inputs(seed: int = 0) -> dict:
    streams_of = jax.random.split(jax.random.key(seed), 6)
    return {
        "tokens": draw_tokens(jax.random.fold_in(streams_of[5], 71), 0),
        "query_weight": bell_draw(streams_of[1], (D, COLS), D ** -0.5, 0.0625, ((0, 32),)),
        "output_weight": bell_draw(streams_of[2], (D, COLS), COLS ** -0.5, 0.0625, ((0, 32),)),
        "keyval_slot": bell_draw(streams_of[3], (N_REP, N_TP, D, 2 * HD), D ** -0.5, 0.0625, ((0, 4), (1, 8))),
        "holder": draw_holder(jax.random.fold_in(streams_of[5], 71), 0),
    }


def reference(tokens, query_weight, output_weight, keyval_slot, holder):
    group = N_TP // KVH
    width = HQW * HD // N_TP
    per_head = HQW // KVH
    scale = 1.0 / math.sqrt(HD)
    rank_ids = jnp.arange(N_TP, dtype=jnp.int32)
    owners = rank_ids // group
    chosen = holder[owners]
    keyval_local = keyval_slot[chosen // group, owners * group + chosen % group]
    head_weights = keyval_local[jnp.arange(KVH, dtype=jnp.int32) * group]
    stacked = jnp.transpose(head_weights, (1, 0, 2)).reshape(D, KVH * 2 * HD)
    keyval_all = jnp.dot(tokens, stacked, preferred_element_type=jnp.float32).astype(jnp.bfloat16)
    query_all = jnp.dot(tokens, query_weight, preferred_element_type=jnp.float32).astype(jnp.bfloat16)
    row_index = lax.broadcasted_iota(jnp.int32, (TOK, TOK), 0)
    col_index = lax.broadcasted_iota(jnp.int32, (TOK, TOK), 1)

    def attend(index):
        owner = index // per_head
        queries = lax.dynamic_slice_in_dim(query_all, index * HD, HD, 1).astype(jnp.float32).reshape(N_REP, TOK, HD)
        keys = lax.dynamic_slice_in_dim(keyval_all, owner * 2 * HD, HD, 1).astype(jnp.float32).reshape(N_REP, TOK, HD)
        values = lax.dynamic_slice_in_dim(keyval_all, owner * 2 * HD + HD, HD, 1).astype(jnp.float32).reshape(N_REP, TOK, HD)
        scores = jnp.einsum('rqd,rkd->rqk', queries, keys) * scale
        scores = jnp.where(col_index <= row_index, scores, -1e+30)
        peak = lax.optimization_barrier(jnp.max(scores, axis=-1, keepdims=True))
        weights = jnp.exp(scores - peak)
        weights = (weights / lax.optimization_barrier(jnp.sum(weights, axis=-1, keepdims=True))).astype(jnp.bfloat16)
        context = jnp.einsum('rqk,rkd->rqd', weights.astype(jnp.float32), values)
        return context.astype(jnp.bfloat16)
    contexts = lax.map(attend, jnp.arange(HQW, dtype=jnp.int32))
    context = jnp.transpose(contexts, (1, 2, 0, 3)).reshape(N_REP * TOK, HQW * HD)

    def add_rank(total, rank):
        context_part = lax.dynamic_slice_in_dim(context, rank * width, width, 1)
        weight_part = lax.dynamic_slice_in_dim(output_weight, rank * width, width, 1)
        term = lax.dot_general(context_part, weight_part, (((1,), (1,)), ((), ())), preferred_element_type=jnp.float32)
        rounded = lax.optimization_barrier(term.astype(jnp.bfloat16))
        return (total + rounded.astype(jnp.float32), None)
    start = jnp.zeros((N_REP * TOK, D), jnp.float32)
    summed, unused = lax.scan(add_rank, start, rank_ids)
    attended = summed.astype(jnp.bfloat16)
    return (query_weight, output_weight, keyval_local, attended)
```

```python
import math

import jax
import jax.numpy as jnp
from jax import lax
from jax.sharding import PartitionSpec as P

HD = 128
KVH = 8
CUTS = 2


def partner_2(block, axis, distance):
    count = lax.axis_size(axis)
    route = []
    for low in range(count):
        high = low | 1 << distance
        if high != low and high < count:
            route += [(low, high), (high, low)]
    return lax.ppermute(block, axis, route)


def after(value, *earlier):
    return lax.optimization_barrier((value, *earlier))[0]


def pick(mask, value, other):
    here = lax.axis_index("rep")
    hit = here < 0
    for replica in mask:
        hit = hit | (here == replica)
    return jnp.where(hit, value, other)


def line_steps(count):
    slots = [{} for _ in range(count - 1)]
    for here in range(count):
        order = []
        for step in range(1, count):
            order += [(step, 0)] if here >= step else []
            order += [(step, 1)] if here + step < count else []
        for slot, key in enumerate(order):
            slots[slot].setdefault(key, []).append(here)
    return slots


def step_right(block, step):
    count = lax.axis_size("rep")
    return lax.ppermute(block, "rep", [(i, i + 1) for i in range(step - 1, count - 1)])


def step_left(block, step):
    count = lax.axis_size("rep")
    return lax.ppermute(block, "rep", [(i, i - 1) for i in range(1, count - step + 1)])


def slot_block(arrived, slot):
    here = lax.axis_index("rep")
    value, origin = None, None
    for (step, side), replicas in slot.items():
        got = arrived[step, side]
        start = here + step if side else here - step
        value = got if value is None else pick(replicas, got, value)
        origin = start if origin is None else pick(replicas, start, origin)
    return value, origin


def keyval_spread(own, home):
    count = lax.axis_size("rep")
    here = lax.axis_index("rep")
    held = own
    for step in range(count - 1):
        down = count - 1 - step
        pairs = [(step, step + 1), (down, down - 1)]
        routes = [pairs] if step + 1 != down - 1 else [pairs[:1], pairs[1:]]
        old = held
        for route in routes:
            got = lax.ppermute(old, "rep", route)
            take = here < 0
            if pairs[0] in route:
                take = take | ((here == step + 1) & (home <= step))
            if pairs[1] in route:
                take = take | ((here == down - 1) & (home >= down))
            held = jnp.where(take, got, held)
    return held


def per_device(tokens, query_weight, output_weight, keyval_slot, holder):
    ranks = lax.axis_size("tp")
    replicas = lax.axis_size("rep")
    here = lax.axis_index("rep")
    height, full = query_weight.shape
    width = full // ranks
    tall = height // CUTS
    slots = line_steps(replicas)

    group = ranks // KVH
    my_rank = lax.axis_index("tp")
    chosen = holder[my_rank // group]
    home_place = chosen % group
    my_place = my_rank % group

    def by_rank(matrix, cut):
        rows = matrix[cut * tall:(cut + 1) * tall].reshape(tall, ranks, width)
        rows = jnp.transpose(rows, (1, 0, 2))
        return lax.all_to_all(rows, "tp", split_axis=0, concat_axis=0, tiled=True)

    def put(whole, block, origin, cut):
        return lax.dynamic_update_slice(whole, block[None, :, None], (origin, 0, cut, 0, 0))

    spread = keyval_spread(keyval_slot[0, 0], chosen // group)
    for level in range(group.bit_length() - 1):
        partner = partner_2(spread, "tp", level)
        holding = (my_place ^ home_place) >> level == 0
        spread = jnp.where(holding, spread, partner)
    piece = lax.all_gather(tokens, "tp", axis=1, tiled=True)

    mine = {}
    last = None
    for name, matrix in (("q", query_weight), ("o", output_weight)):
        for cut in range(CUTS):
            mine[name, cut] = by_rank(matrix if last is None else after(matrix, last), cut)
            last = mine[name, cut]
    arrived = {}
    order = [(name, step, cut) for name in "qo" for step in range(1, replicas) for cut in range(CUTS)]
    gate = []
    for name, step, cut in order:
        chain = arrived.setdefault((name, cut), {})
        right = chain[step - 1, 0] if step > 1 else mine[name, cut]
        left = chain[step - 1, 1] if step > 1 else mine[name, cut]
        if len(gate) >= 2 * CUTS:
            early = gate[-2 * CUTS]
            if step == 1:
                right, left = lax.optimization_barrier((right, left, *early))[:2]
        chain[step, 0] = step_right(right, step)
        chain[step, 1] = step_left(left, step)
        gate.append((chain[step, 0], chain[step, 1]))

    def assemble(name):
        whole = jnp.zeros((replicas, ranks, CUTS, tall, width), jnp.bfloat16)
        parts = []
        for cut in range(CUTS):
            whole = put(whole, mine[name, cut], here, cut)
            parts.append((mine[name, cut], here, cut))
        for slot in slots:
            for cut in range(CUTS):
                block, origin = slot_block(arrived[name, cut], slot)
                whole = put(whole, block, origin, cut)
                parts.append((block, origin, cut))
        return whole.reshape(-1, width), parts

    query_local, _ = assemble("q")
    output_local, output_parts = assemble("o")

    token_count = tokens.shape[0]
    query_sum = jnp.dot(piece, query_local, preferred_element_type=jnp.float32)
    keyval_sum = jnp.dot(piece, spread, preferred_element_type=jnp.float32)
    heads_local = width // HD
    queries = query_sum.astype(jnp.bfloat16).reshape(token_count, heads_local, HD)
    keyval = keyval_sum.astype(jnp.bfloat16)
    keys = keyval[:, :HD]
    values = keyval[:, HD:]
    scale = 1.0 / math.sqrt(HD)
    scores = jnp.einsum("qhd,kd->hqk", queries, keys, preferred_element_type=jnp.float32) * scale
    row_index = lax.broadcasted_iota(jnp.int32, (token_count, token_count), 0)
    col_index = lax.broadcasted_iota(jnp.int32, (token_count, token_count), 1)
    scores = jnp.where(col_index <= row_index, scores, -1e30)
    peak = jnp.max(scores, axis=-1, keepdims=True)
    weights = jnp.exp(scores - peak)
    weights = (weights / jnp.sum(weights, axis=-1, keepdims=True)).astype(jnp.bfloat16)
    context = jnp.einsum("hqk,kd->qhd", weights, values, preferred_element_type=jnp.float32)
    context = context.astype(jnp.bfloat16).reshape(token_count, width)

    share = token_count // ranks
    attended = jnp.zeros((share, replicas, ranks, CUTS, tall), jnp.bfloat16)
    for block, origin, cut in output_parts:
        partial = lax.dot_general(
            context, block.reshape(-1, width), (((1,), (1,)), ((), ())),
            preferred_element_type=jnp.float32,
        ).astype(jnp.bfloat16)
        summed = lax.psum_scatter(partial, "tp", scatter_dimension=0, tiled=True)
        attended = lax.dynamic_update_slice(
            attended, summed.reshape(share, 1, ranks, 1, tall), (0, origin, 0, cut, 0)
        )
    return (
        query_local,
        output_local,
        spread.reshape(1, spread.shape[0], spread.shape[1]),
        attended.reshape(share, -1),
    )


def solution(mesh):
    in_specs = (
        P("rep", "tp"),
        P(("rep", "tp"), None),
        P(("rep", "tp"), None),
        P("rep", "tp", None, None),
        P(),
    )
    out_specs = (P(None, "tp"), P(None, "tp"), P("tp", None, None), P(("rep", "tp"), None))
    return jax.shard_map(
        per_device, mesh=mesh, in_specs=in_specs, out_specs=out_specs, check_vma=False
    )
```

```python
import math

import jax
import jax.numpy as jnp
from jax import lax
from jax.sharding import PartitionSpec as P

HD = 128
KVH = 8
CUTS = 2


def partner_2(block, axis, distance):
    count = lax.axis_size(axis)
    route = []
    for low in range(count):
        high = low | 1 << distance
        if high != low and high < count:
            route += [(low, high), (high, low)]
    return lax.ppermute(block, axis, route)


def after(value, *earlier):
    return lax.optimization_barrier((value, *earlier))[0]


def pick(mask, value, other):
    here = lax.axis_index("rep")
    hit = here < 0
    for replica in mask:
        hit = hit | (here == replica)
    return jnp.where(hit, value, other)


def line_steps(count):
    slots = [{} for _ in range(count - 1)]
    for here in range(count):
        order = []
        for step in range(1, count):
            order += [(step, 0)] if here >= step else []
            order += [(step, 1)] if here + step < count else []
        for slot, key in enumerate(order):
            slots[slot].setdefault(key, []).append(here)
    return slots


def step_right(block, step):
    count = lax.axis_size("rep")
    return lax.ppermute(block, "rep", [(i, i + 1) for i in range(step - 1, count - 1)])


def step_left(block, step):
    count = lax.axis_size("rep")
    return lax.ppermute(block, "rep", [(i, i - 1) for i in range(1, count - step + 1)])


def slot_block(arrived, slot):
    here = lax.axis_index("rep")
    value, origin = None, None
    for (step, side), replicas in slot.items():
        got = arrived[step, side]
        start = here + step if side else here - step
        value = got if value is None else pick(replicas, got, value)
        origin = start if origin is None else pick(replicas, start, origin)
    return value, origin


def keyval_spread(own, home):
    count = lax.axis_size("rep")
    here = lax.axis_index("rep")
    held = own
    for step in range(count - 1):
        down = count - 1 - step
        pairs = [(step, step + 1), (down, down - 1)]
        routes = [pairs] if step + 1 != down - 1 else [pairs[:1], pairs[1:]]
        old = held
        for route in routes:
            got = lax.ppermute(old, "rep", route)
            take = here < 0
            if pairs[0] in route:
                take = take | ((here == step + 1) & (home <= step))
            if pairs[1] in route:
                take = take | ((here == down - 1) & (home >= down))
            held = jnp.where(take, got, held)
    return held


def per_device(tokens, query_weight, output_weight, keyval_slot, holder):
    ranks = lax.axis_size("tp")
    replicas = lax.axis_size("rep")
    here = lax.axis_index("rep")
    height, full = query_weight.shape
    width = full // ranks
    tall = height // CUTS
    slots = line_steps(replicas)

    group = ranks // KVH
    my_rank = lax.axis_index("tp")
    chosen = holder[my_rank // group]
    home_place = chosen % group
    my_place = my_rank % group

    def across(rows):
        rows = jnp.transpose(rows.reshape(tall, ranks, width), (1, 0, 2))
        return lax.all_to_all(rows, "tp", split_axis=0, concat_axis=0, tiled=True)

    def rows_of(matrix, cut):
        return matrix[cut * tall:(cut + 1) * tall]

    mine = {("q", 0): rows_of(query_weight, 0)}
    last = ()
    for name, matrix, cut in [("q", query_weight, 1), ("o", output_weight, 0), ("o", output_weight, 1)]:
        mine[name, cut] = across(rows_of(after(matrix, *last) if last else matrix, cut))
        last = (mine[name, cut],)
    piece = lax.all_gather(after(tokens, mine["q", 1]), "tp", axis=1, tiled=True)

    arrived = {}

    def advance(name, cut, step, *earlier):
        chain = arrived.setdefault((name, cut), {})
        right = chain[step - 1, 0] if step > 1 else mine[name, cut]
        left = chain[step - 1, 1] if step > 1 else mine[name, cut]
        if earlier:
            right, left = lax.optimization_barrier((right, left, *earlier))[:2]
        chain[step, 0] = step_right(right, step)
        chain[step, 1] = step_left(left, step)

    def landed(name, cut, step):
        return arrived[name, cut][step, 0], arrived[name, cut][step, 1]

    final = replicas - 1
    for step in range(1, replicas):
        for cut in range(CUTS):
            advance("q", cut, step)
    spread = keyval_spread(keyval_slot[0, 0], chosen // group)
    for step in range(1, replicas):
        for cut in range(CUTS):
            wait = ()
            if step == 1:
                wait = (spread,) if cut else landed("q", CUTS - 1, final)
            advance("o", cut, step, *wait)
    for level in range(group.bit_length() - 1):
        partner = partner_2(spread, "tp", level)
        holding = (my_place ^ home_place) >> level == 0
        spread = jnp.where(holding, spread, partner)
    piece = after(piece, *landed("o", 0, max(final - 1, 1)))

    def put(whole, block, origin, cut):
        return lax.dynamic_update_slice(whole, block[None, :, None], (origin, 0, cut, 0, 0))

    def assemble(name):
        whole = jnp.zeros((replicas, ranks, CUTS, tall, width), jnp.bfloat16)
        parts = []
        for slot in [None] + slots:
            blocks = []
            for cut in range(CUTS):
                if slot is None:
                    block, origin = mine[name, cut], here
                else:
                    block, origin = slot_block(arrived[name, cut], slot)
                if (name, cut) == ("q", 0):
                    block = across(block)
                whole = put(whole, block, origin, cut)
                blocks.append(block)
            parts.append((blocks, origin))
        return whole.reshape(-1, width), parts

    query_local, _ = assemble("q")
    output_local, output_parts = assemble("o")

    token_count = tokens.shape[0]
    query_sum = jnp.dot(piece, query_local, preferred_element_type=jnp.float32)
    keyval_sum = jnp.dot(piece, spread, preferred_element_type=jnp.float32)
    heads_local = width // HD
    queries = query_sum.astype(jnp.bfloat16).reshape(token_count, heads_local, HD)
    keyval = keyval_sum.astype(jnp.bfloat16)
    keys = keyval[:, :HD]
    values = keyval[:, HD:]
    scale = 1.0 / math.sqrt(HD)
    scores = jnp.einsum("qhd,kd->hqk", queries, keys, preferred_element_type=jnp.float32) * scale
    row_index = lax.broadcasted_iota(jnp.int32, (token_count, token_count), 0)
    col_index = lax.broadcasted_iota(jnp.int32, (token_count, token_count), 1)
    scores = jnp.where(col_index <= row_index, scores, -1e30)
    peak = jnp.max(scores, axis=-1, keepdims=True)
    weights = jnp.exp(scores - peak)
    weights = (weights / jnp.sum(weights, axis=-1, keepdims=True)).astype(jnp.bfloat16)
    context = jnp.einsum("hqk,kd->qhd", weights, values, preferred_element_type=jnp.float32)
    context = context.astype(jnp.bfloat16).reshape(token_count, width)

    share = token_count // ranks
    attended = jnp.zeros((share, full), jnp.bfloat16)
    span = ranks * height

    def project(block):
        return lax.dot_general(
            context, block.reshape(-1, width), (((1,), (1,)), ((), ())),
            preferred_element_type=jnp.float32,
        ).astype(jnp.bfloat16)

    for position, (blocks, origin) in enumerate(output_parts):
        if position < len(output_parts) - 1:
            partial = project(jnp.stack(blocks, axis=1))
            summed = lax.psum_scatter(partial, "tp", scatter_dimension=0, tiled=True)
        else:
            sums = []
            for block in blocks:
                terms = project(block).reshape(ranks, share, -1)
                terms = lax.all_to_all(terms, "tp", split_axis=0, concat_axis=0, tiled=True)
                total = jnp.sum(terms.astype(jnp.float32), axis=0).astype(jnp.bfloat16)
                sums.append(total.reshape(share, ranks, tall))
            summed = jnp.stack(sums, axis=2).reshape(share, span)
        attended = lax.dynamic_update_slice(attended, summed, (0, origin * span))
    return (
        query_local,
        output_local,
        spread.reshape(1, spread.shape[0], spread.shape[1]),
        attended,
    )


def solution(mesh):
    in_specs = (
        P("rep", "tp"),
        P(("rep", "tp"), None),
        P(("rep", "tp"), None),
        P("rep", "tp", None, None),
        P(),
    )
    out_specs = (P(None, "tp"), P(None, "tp"), P("tp", None, None), P(("rep", "tp"), None))
    return jax.shard_map(
        per_device, mesh=mesh, in_specs=in_specs, out_specs=out_specs, check_vma=False
    )
```

```python
import math

import jax
import jax.numpy as jnp
from jax import lax
from jax.sharding import PartitionSpec as P

HD = 128
KVH = 8
CUTS = 2


def partner_2(block, axis, distance):
    count = lax.axis_size(axis)
    route = []
    for low in range(count):
        high = low | 1 << distance
        if high != low and high < count:
            route += [(low, high), (high, low)]
    return lax.ppermute(block, axis, route)


def after(value, *earlier):
    return lax.optimization_barrier((value, *earlier))[0]


def pick(mask, value, other):
    here = lax.axis_index("rep")
    hit = here < 0
    for replica in mask:
        hit = hit | (here == replica)
    return jnp.where(hit, value, other)


def line_steps(count):
    slots = [{} for _ in range(count - 1)]
    for here in range(count):
        order = []
        for step in range(1, count):
            order += [(step, 0)] if here >= step else []
            order += [(step, 1)] if here + step < count else []
        for slot, key in enumerate(order):
            slots[slot].setdefault(key, []).append(here)
    return slots


def step_right(block, step):
    count = lax.axis_size("rep")
    return lax.ppermute(block, "rep", [(i, i + 1) for i in range(step - 1, count - 1)])


def step_left(block, step):
    count = lax.axis_size("rep")
    return lax.ppermute(block, "rep", [(i, i - 1) for i in range(1, count - step + 1)])


def slot_block(arrived, slot):
    here = lax.axis_index("rep")
    value, origin = None, None
    for (step, side), replicas in slot.items():
        got = arrived[step, side]
        start = here + step if side else here - step
        value = got if value is None else pick(replicas, got, value)
        origin = start if origin is None else pick(replicas, start, origin)
    return value, origin


def keyval_spread(own, home):
    count = lax.axis_size("rep")
    here = lax.axis_index("rep")
    held = own
    for step in range(count - 1):
        down = count - 1 - step
        pairs = [(step, step + 1), (down, down - 1)]
        routes = [pairs] if step + 1 != down - 1 else [pairs[:1], pairs[1:]]
        old = held
        for route in routes:
            got = lax.ppermute(old, "rep", route)
            take = here < 0
            if pairs[0] in route:
                take = take | ((here == step + 1) & (home <= step))
            if pairs[1] in route:
                take = take | ((here == down - 1) & (home >= down))
            held = jnp.where(take, got, held)
    return held


def per_device(tokens, query_weight, output_weight, keyval_slot, holder):
    ranks = lax.axis_size("tp")
    replicas = lax.axis_size("rep")
    here = lax.axis_index("rep")
    height, full = query_weight.shape
    width = full // ranks
    tall = height // CUTS
    slots = line_steps(replicas)

    group = ranks // KVH
    my_rank = lax.axis_index("tp")
    chosen = holder[my_rank // group]
    home_place = chosen % group
    my_place = my_rank % group

    def across(rows):
        rows = jnp.transpose(rows.reshape(tall, ranks, width), (1, 0, 2))
        return lax.all_to_all(rows, "tp", split_axis=0, concat_axis=0, tiled=True)

    def rows_of(matrix, cut):
        return matrix[cut * tall:(cut + 1) * tall]

    mine = {("q", 0): rows_of(query_weight, 0)}
    last = ()
    for name, matrix, cut in [("q", query_weight, 1), ("o", output_weight, 0), ("o", output_weight, 1)]:
        mine[name, cut] = across(after(rows_of(matrix, cut), *last))
        last = (mine[name, cut],)
    piece = lax.all_gather(after(tokens, mine["q", 1]), "tp", axis=1, tiled=True)

    arrived = {}

    def advance(name, cut, step, *earlier):
        chain = arrived.setdefault((name, cut), {})
        right = chain[step - 1, 0] if step > 1 else mine[name, cut]
        left = chain[step - 1, 1] if step > 1 else mine[name, cut]
        if earlier:
            right, left = lax.optimization_barrier((right, left, *earlier))[:2]
        chain[step, 0] = step_right(right, step)
        chain[step, 1] = step_left(left, step)

    def landed(name, cut, step):
        return arrived[name, cut][step, 0], arrived[name, cut][step, 1]

    final = replicas - 1
    for step in range(1, replicas):
        for cut in range(CUTS):
            advance("q", cut, step)
    spread = keyval_spread(keyval_slot[0, 0], chosen // group)
    for step in range(1, replicas):
        for cut in range(CUTS):
            wait = ()
            if step == 1:
                wait = (spread,) if cut else landed("q", CUTS - 1, final)
            advance("o", cut, step, *wait)
    for level in range(group.bit_length() - 1):
        partner = partner_2(spread, "tp", level)
        holding = (my_place ^ home_place) >> level == 0
        spread = jnp.where(holding, spread, partner)
    piece = after(piece, *landed("o", 0, max(final - 1, 1)))

    def put(whole, block, origin, cut):
        return lax.dynamic_update_slice(whole, block[None, :, None], (origin, 0, cut, 0, 0))

    def assemble(name):
        whole = jnp.zeros((replicas, ranks, CUTS, tall, width), jnp.bfloat16)
        parts = []
        for slot in [None] + slots:
            blocks = []
            for cut in range(CUTS):
                if slot is None:
                    block, origin = mine[name, cut], here
                else:
                    block, origin = slot_block(arrived[name, cut], slot)
                if (name, cut) == ("q", 0):
                    block = across(block)
                whole = put(whole, block, origin, cut)
                blocks.append(block)
            parts.append((blocks, origin))
        return whole.reshape(-1, width), parts

    query_local, _ = assemble("q")
    output_local, output_parts = assemble("o")

    token_count = tokens.shape[0]
    query_sum = jnp.dot(piece, query_local, preferred_element_type=jnp.float32)
    keyval_sum = jnp.dot(piece, spread, preferred_element_type=jnp.float32)
    heads_local = width // HD
    queries = query_sum.astype(jnp.bfloat16).reshape(token_count, heads_local, HD)
    keyval = keyval_sum.astype(jnp.bfloat16)
    keys = keyval[:, :HD]
    values = keyval[:, HD:]
    scale = 1.0 / math.sqrt(HD)
    scores = jnp.einsum("qhd,kd->hqk", queries, keys, preferred_element_type=jnp.float32) * scale
    row_index = lax.broadcasted_iota(jnp.int32, (token_count, token_count), 0)
    col_index = lax.broadcasted_iota(jnp.int32, (token_count, token_count), 1)
    scores = jnp.where(col_index <= row_index, scores, -1e30)
    peak = jnp.max(scores, axis=-1, keepdims=True)
    weights = jnp.exp(scores - peak)
    weights = (weights / jnp.sum(weights, axis=-1, keepdims=True)).astype(jnp.bfloat16)
    context = jnp.einsum("hqk,kd->qhd", weights, values, preferred_element_type=jnp.float32)
    context = context.astype(jnp.bfloat16).reshape(token_count, width)

    share = token_count // ranks
    attended = jnp.zeros((share, full), jnp.bfloat16)
    span = ranks * height

    def project(block):
        return lax.dot_general(
            context, block.reshape(-1, width), (((1,), (1,)), ((), ())),
            preferred_element_type=jnp.float32,
        ).astype(jnp.bfloat16)

    for blocks, origin in output_parts:
        sums = []
        for block in blocks:
            terms = project(block).reshape(ranks, share, -1)
            terms = lax.all_to_all(terms, "tp", split_axis=0, concat_axis=0, tiled=True)
            total = jnp.sum(terms.astype(jnp.float32), axis=0).astype(jnp.bfloat16)
            sums.append(total.reshape(share, ranks, tall))
        summed = jnp.stack(sums, axis=2).reshape(share, span)
        attended = lax.dynamic_update_slice(attended, summed, (0, origin * span))
    return (
        query_local,
        output_local,
        spread.reshape(1, spread.shape[0], spread.shape[1]),
        attended,
    )


def solution(mesh):
    in_specs = (
        P("rep", "tp"),
        P(("rep", "tp"), None),
        P(("rep", "tp"), None),
        P("rep", "tp", None, None),
        P(),
    )
    out_specs = (P(None, "tp"), P(None, "tp"), P("tp", None, None), P(("rep", "tp"), None))
    return jax.shard_map(
        per_device, mesh=mesh, in_specs=in_specs, out_specs=out_specs, check_vma=False
    )
```
